32 devices in a mesh: replica: 4 (over z), tensor: 8 (over y, x, core).
Axes of the slice: x: 2, y: 2, z: 4, core: 2. Of those that a mesh axis runs over, the one named last changes fastest.
Arguments:
- hidden_input: bfloat16 [640, 2, 8192], P('replica', None, 'tensor'), may hold values from -200 to 200
- input_norm_gain: bfloat16 [8192], replicated, may hold values from 0.099609375 to 1.8984375
- merged_weight: bfloat16 [8192, 6144], P(None, 'tensor'), may hold values from -0.0625 to 0.0625
- output_weight: bfloat16 [4096, 8192], P('tensor'), may hold values from -0.375 to 0.375
- adapter_down: bfloat16 [256, 16, 8192], P('replica', None, 'tensor'), may hold values from -0.0625 to 0.0625
- adapter_up: bfloat16 [256, 16, 6144], P('replica', None, 'tensor'), may hold values from -0.75 to 0.75
- request_adapter: int32 [640], replicated, may hold values from 0 to 255
- key_value_cache: bfloat16 [5120, 16, 2048], P(('replica', 'tensor')), may hold values from -1000 to 1000
- block_table: int32 [640, 8], P(('replica', 'tensor')), may hold values from 0 to 159, as said below
- cache_length: int32 [640], P(('replica', 'tensor')), may hold values from 1 to 128, as said below
- partner: int32 [4, 8], replicated, may hold values from 0 to 3, as said below
- moving: int32 [640], P(('replica', 'tensor')), may hold values from 0 to 1, as said below
Outputs:
- attn_out: bfloat16 [640, 2, 8192], P('replica', None, 'tensor')
- arrived_kv: bfloat16 [64, 128, 2048], P(('replica', 'tensor'))
The draws below stay inside these ranges and needn't reach their ends.
Inputs may be any that keep to these rules, and one draw needn't show every extreme that they name: `block_table`: the rows of one device (the 20 home slots of one replica and one tensor index) hold every block index of 0 to 159 exactly once. `cache_length`: among the 20 requests of one device one has all 128 positions cached. partner[r, k] = r XOR m_k for one m_k of 1 to 3 for each tensor index k, the same for every replica. Slot s of replica r moves exactly when slot s of replica partner[r, s // 20] does. Each device's 20 slots hold 1 to 2 moving ones, and some device holds 2.
All inputs are finite; a program needn't handle non-finite values.
Results may differ from the reference program's by a relative error of at most 0.035.
Values may be sent and summed in bfloat16 or wider, within the bound.
A program may use at most 256 MiB of HBM per device.

```python
import math
import jax
import jax.numpy as jnp
import numpy as np
from jax import lax

EMBED_WIDTH = 8192
QUERY_HEADS = 32
KEY_VALUE_HEADS = 8
HEAD_SIZE = 128
ADAPTER_RANK = 16
ADAPTER_TOTAL = 256
FRESH_TOKENS = 2
BLK = 16
MAXB = 8
MIG_DEV = 2
REQUESTS_LOCAL = 20
MERGED_COLUMNS = 6144
LMAX = 128
REPLICAS = 4
TENSORS = 8
B = 160
REQUEST_TOTAL = 640
NBLK_DEV = 160
POOL = 5120
N_TENSOR = 8


def draw_hidden_input(key, part):
    values = jnp.clip(jax.random.normal(key, (REQUEST_TOTAL, FRESH_TOKENS, EMBED_WIDTH), jnp.float32), -6.0, 6.0)
    return values.astype(jnp.bfloat16)


def draw_key_value_cache(key, part):
    track_count = 2 * KEY_VALUE_HEADS * HEAD_SIZE
    shape_all = (POOL, BLK, track_count)
    values = jax.random.normal(key, shape_all, jnp.float32)
    return jnp.clip(values, -1000.0, 1000.0).astype(jnp.bfloat16)


def draw_block_table(key, part):
    device_keys = jax.random.split(key, REPLICAS * TENSORS)
    orders = jax.vmap(lambda single_key: jax.random.permutation(single_key, NBLK_DEV))(device_keys)
    return orders.reshape(REQUEST_TOTAL, MAXB).astype(jnp.int32)


def draw_cache_length(key, part):
    lengths = jax.random.randint(key, (REPLICAS * TENSORS, REQUESTS_LOCAL), 1, LMAX + 1)
    full_at = jax.random.randint(jax.random.fold_in(key, 21), (REPLICAS * TENSORS, 1), 0, REQUESTS_LOCAL)
    lengths = jnp.where(jnp.arange(REQUESTS_LOCAL, dtype=jnp.int32)[None, :] == full_at, LMAX, lengths)
    return lengths.reshape(REQUEST_TOTAL).astype(jnp.int32)


def pair_mask(key):
    return jax.random.randint(jax.random.fold_in(key, 11), (TENSORS,), 1, REPLICAS).astype(jnp.int32)


def draw_partner(key, part):
    flip_bits = pair_mask(key)
    replica_ids = jnp.arange(REPLICAS, dtype=jnp.int32)
    return jnp.bitwise_xor(replica_ids[:, None], flip_bits[None, :]).astype(jnp.int32)


def draw_moving(key, part):
    flip_bits = pair_mask(key)
    counts = jax.random.randint(jax.random.fold_in(key, 12), (REPLICAS, TENSORS), 1, MIG_DEV + 1)
    full_at = jax.random.randint(jax.random.fold_in(key, 13), (REPLICAS, 1), 0, TENSORS)
    counts = jnp.where(jnp.arange(TENSORS, dtype=jnp.int32)[None, :] == full_at, MIG_DEV, counts)
    device_keys = jax.random.split(jax.random.fold_in(key, 14), REPLICAS * TENSORS)
    orders = jax.vmap(lambda single_key: jax.random.permutation(single_key, REQUESTS_LOCAL))(device_keys)
    ranks = jnp.argsort(orders, axis=-1).reshape(REPLICAS, TENSORS, REQUESTS_LOCAL)
    chosen = (ranks < counts[:, :, None]).astype(jnp.int32)
    replica_ids = jnp.arange(REPLICAS, dtype=jnp.int32)
    lower = jnp.minimum(replica_ids[:, None], jnp.bitwise_xor(replica_ids[:, None], flip_bits[None, :]))
    tensor_ids = jnp.arange(TENSORS, dtype=jnp.int32)[None, :]
    return chosen[lower, tensor_ids].reshape(REQUEST_TOTAL).astype(jnp.int32)


def place_ends(values, own_key, smallest, largest):
    shape = values.shape
    spot = [jax.random.randint(jax.random.fold_in(own_key, axis), (), 0, shape[axis]) for axis in range(len(shape))]
    values = values.at[tuple(spot)].set(smallest)
    longest = shape.index(max(shape))
    spot[longest] = (spot[longest] + 1) % shape[longest]
    return values.at[tuple(spot)].set(largest)


def block_scale(rng, dims, pieces, smallest, top_value):
    loudness = 1.0
    for position, blocks in pieces:
        steps = jax.random.uniform(jax.random.fold_in(jax.random.fold_in(rng, 6), position), (blocks,), jnp.float32, smallest / len(pieces), top_value / len(pieces))
        loudness = loudness * jnp.repeat(jnp.exp(steps), dims[position] // blocks).reshape((-1,) + (1,) * (len(dims) - 1 - position))
    return loudness


def rank_table(amount, slope):
    weights = [(1 << 20) // math.isqrt(rank ** slope) + 1 for rank in range(1, amount + 1)]
    width = 1 + sum(weights) // (1 << 30)
    return np.cumsum(np.array([max(1, weight // width) for weight in weights]))


def ranked_ids(rng, shape, amount, slope):
    grid = rank_table(amount, slope)
    lot = jax.random.randint(jax.random.fold_in(rng, 1), shape, 0, int(grid[amount - 1]))
    standing = jnp.searchsorted(jnp.asarray(grid, jnp.int32), lot, side="right")
    return jax.random.permutation(jax.random.fold_in(rng, 2), amount)[standing].astype(jnp.int32)


def bell_draw(key, shape, scale, bound, pieces=(), kind=jnp.bfloat16):
    array = jax.random.normal(key, shape, jnp.float32) * scale
    if len(pieces) > 0:
        array = block_scale(key, shape, pieces, -0.22, 0.18) * array
    return jnp.clip(array, min=-bound, max=bound).astype(kind)


def setup_inputs(seed: int = 0) -> dict:
    streams_of = jax.random.split(jax.random.key(seed), 13)
    return {
        "hidden_input": draw_hidden_input(jax.random.fold_in(streams_of[12], 71), 0),
        "input_norm_gain": jnp.clip(1.0 + 0.18 * jax.random.normal(streams_of[1], (EMBED_WIDTH,), jnp.float32), 0.099609375, 1.8984375).astype(jnp.bfloat16),
        "merged_weight": bell_draw(streams_of[2], (EMBED_WIDTH, MERGED_COLUMNS), EMBED_WIDTH ** -0.5, 0.0625, ((1, 8),)),
        "output_weight": bell_draw(streams_of[3], (QUERY_HEADS * HEAD_SIZE, EMBED_WIDTH), (QUERY_HEADS * HEAD_SIZE // 16) ** -0.5, 0.375, ((0, 8),)),
        "adapter_down": bell_draw(streams_of[4], (ADAPTER_TOTAL, ADAPTER_RANK, EMBED_WIDTH), EMBED_WIDTH ** -0.5, 0.0625, ((0, 4), (2, 8))),
        "adapter_up": bell_draw(streams_of[5], (ADAPTER_TOTAL, ADAPTER_RANK, MERGED_COLUMNS), (4 * ADAPTER_RANK) ** -0.5, 0.75, ((0, 4), (2, 8))),
        "request_adapter": place_ends(ranked_ids(streams_of[6], (REQUEST_TOTAL,), ADAPTER_TOTAL, 2), jax.random.fold_in(streams_of[6], 3), 0, ADAPTER_TOTAL - 1).astype(jnp.int32),
        "key_value_cache": draw_key_value_cache(jax.random.fold_in(streams_of[12], 71), 0),
        "block_table": draw_block_table(jax.random.fold_in(streams_of[12], 71), 0),
        "cache_length": draw_cache_length(jax.random.fold_in(streams_of[12], 71), 0),
        "partner": draw_partner(jax.random.fold_in(streams_of[12], 71), 0),
        "moving": draw_moving(jax.random.fold_in(streams_of[12], 71), 0),
    }


theta_base = 500000.0
norm_eps = 1e-05
adapter_scale = 2.0

def rotate(vectors, positions):
    track_count = vectors.shape[-1]
    half_width = track_count // 2
    frequency = jnp.power(jnp.float32(theta_base), -jnp.arange(half_width, dtype=jnp.float32) / half_width)
    angles = positions.astype(jnp.float32)[..., None] * frequency
    cosine = jnp.cos(angles)
    sine_part = jnp.sin(angles)
    first_half = vectors[..., :half_width].astype(jnp.float32)
    second = vectors[..., half_width:].astype(jnp.float32)
    joined = jnp.concatenate([first_half * cosine - second * sine_part, second * cosine + first_half * sine_part], axis=-1)
    return joined.astype(jnp.bfloat16)

def new_entries(projected_rows, lengths):
    item_count = projected_rows.shape[0]
    fresh_tokens = projected_rows.shape[1]
    query_columns = QUERY_HEADS * HEAD_SIZE
    key_columns = KEY_VALUE_HEADS * HEAD_SIZE
    fresh_keys = projected_rows[:, :, query_columns:query_columns + key_columns].reshape(item_count, fresh_tokens, KEY_VALUE_HEADS, HEAD_SIZE)
    offsets = jnp.arange(fresh_tokens, dtype=jnp.int32)
    positions = lengths[:, None] + offsets[None, :]
    rotated = rotate(fresh_keys, positions[:, :, None]).reshape(item_count, fresh_tokens, key_columns)
    fresh_values = projected_rows[:, :, query_columns + key_columns:]
    return jnp.concatenate([rotated, fresh_values], axis=-1)

def append_cache(key_value_blocks, entries, lengths, live):
    span = key_value_blocks.shape[1]
    places = jnp.arange(span, dtype=jnp.int32)[None, :]
    kept = jnp.where((places < lengths[:, None])[:, :, None], key_value_blocks, jnp.zeros((), key_value_blocks.dtype))
    for offset in range(entries.shape[1]):
        written = (places == lengths[:, None] + offset)[:, :, None]
        kept = jnp.where(written, entries[:, offset][:, None, :], kept)
    return jnp.where(live[:, None, None], kept, jnp.zeros((), kept.dtype))

def attend(projected_rows, key_value_blocks, lengths):
    item_count = projected_rows.shape[0]
    fresh_tokens = projected_rows.shape[1]
    head_sharing = QUERY_HEADS // KEY_VALUE_HEADS
    cache_extent = key_value_blocks.shape[1]
    query_columns = QUERY_HEADS * HEAD_SIZE
    key_columns = KEY_VALUE_HEADS * HEAD_SIZE
    query_rows = projected_rows[:, :, :query_columns].reshape(item_count, fresh_tokens, KEY_VALUE_HEADS, head_sharing, HEAD_SIZE)
    fresh_keys = projected_rows[:, :, query_columns:query_columns + key_columns].reshape(item_count, fresh_tokens, KEY_VALUE_HEADS, HEAD_SIZE)
    fresh_values = projected_rows[:, :, query_columns + key_columns:].reshape(item_count, fresh_tokens, KEY_VALUE_HEADS, HEAD_SIZE).astype(jnp.float32)
    offsets = jnp.arange(fresh_tokens, dtype=jnp.int32)
    positions = lengths[:, None] + offsets[None, :]
    query_rows = rotate(query_rows, positions[:, :, None, None]).astype(jnp.float32)
    fresh_keys = rotate(fresh_keys, positions[:, :, None]).astype(jnp.float32)
    prior_keys = key_value_blocks[:, :, :key_columns].reshape(item_count, cache_extent, KEY_VALUE_HEADS, HEAD_SIZE).astype(jnp.float32)
    prior_values = key_value_blocks[:, :, key_columns:].reshape(item_count, cache_extent, KEY_VALUE_HEADS, HEAD_SIZE).astype(jnp.float32)
    scaling = HEAD_SIZE ** (-0.5)
    old_scores = jnp.einsum('nthgd,nlhd->nthgl', query_rows, prior_keys) * scaling
    new_scores = jnp.einsum('nthgd,nshd->nthgs', query_rows, fresh_keys) * scaling
    old_valid = jnp.arange(cache_extent, dtype=jnp.int32)[None, :] < lengths[:, None]
    new_valid = offsets[None, :] <= offsets[:, None]
    old_scores = jnp.where(old_valid[:, None, None, None, :], old_scores, -jnp.inf)
    new_scores = jnp.where(new_valid[None, :, None, None, :], new_scores, -jnp.inf)
    highest = jnp.maximum(lax.optimization_barrier(jnp.max(old_scores, axis=-1)), lax.optimization_barrier(jnp.max(new_scores, axis=-1)))
    old_exp = jnp.exp(old_scores - highest[..., None])
    new_exp = jnp.exp(new_scores - highest[..., None])
    totals = lax.optimization_barrier(jnp.sum(old_exp, axis=-1)) + lax.optimization_barrier(jnp.sum(new_exp, axis=-1))
    old_weights = (old_exp / totals[..., None]).astype(jnp.bfloat16).astype(jnp.float32)
    new_weights = (new_exp / totals[..., None]).astype(jnp.bfloat16).astype(jnp.float32)
    mixed = jnp.einsum('nthgl,nlhd->nthgd', old_weights, prior_values) + jnp.einsum('nthgs,nshd->nthgd', new_weights, fresh_values)
    return mixed.reshape(item_count, fresh_tokens, QUERY_HEADS * HEAD_SIZE).astype(jnp.bfloat16)

def reference(hidden_input, input_norm_gain, merged_weight, output_weight, adapter_down, adapter_up, request_adapter, key_value_cache, block_table, cache_length, partner, moving):
    hidden_f = hidden_input.astype(jnp.float32)
    mean_square = lax.optimization_barrier(jnp.mean(hidden_f * hidden_f, axis=-1, keepdims=True))
    normed_hidden = (hidden_f * lax.rsqrt(mean_square + norm_eps) * input_norm_gain.astype(jnp.float32)).astype(jnp.bfloat16)
    base_projection = jnp.dot(normed_hidden.reshape(-1, EMBED_WIDTH), merged_weight, preferred_element_type=jnp.float32).reshape(REQUEST_TOTAL, FRESH_TOKENS, MERGED_COLUMNS)
    group_total = REQUEST_TOTAL // REQUESTS_LOCAL

    def adapter_block(input_values):
        rows_block, block_index_list = input_values
        down_weight_rows = adapter_down[block_index_list].astype(jnp.float32)
        shrink = jnp.einsum('bnd,brd->bnr', rows_block.astype(jnp.float32), down_weight_rows)
        shrink_low = lax.optimization_barrier(shrink.astype(jnp.bfloat16))
        up_weight_rows = adapter_up[block_index_list].astype(jnp.float32)
        return jnp.einsum('bnr,brc->bnc', shrink_low.astype(jnp.float32), up_weight_rows)
    widen_step = lax.map(adapter_block, (normed_hidden.reshape(group_total, REQUESTS_LOCAL, FRESH_TOKENS, EMBED_WIDTH), request_adapter.reshape(group_total, REQUESTS_LOCAL)))
    projected_rows = (base_projection + adapter_scale * widen_step.reshape(REQUEST_TOTAL, FRESH_TOKENS, MERGED_COLUMNS)).astype(jnp.bfloat16)
    slots = jnp.arange(REQUEST_TOTAL, dtype=jnp.int32)
    replica_of = slots // B
    tensor_of = slots % B // REQUESTS_LOCAL
    home = jnp.where(moving == 1, partner[replica_of, tensor_of], replica_of).astype(jnp.int32)
    home_slot = (home * B + slots % B).astype(jnp.int32)
    block_ids = ((home_slot // REQUESTS_LOCAL)[:, None] * NBLK_DEV + block_table[home_slot]).astype(jnp.int32)
    track_count = key_value_cache.shape[2]

    def attend_block(input_values):
        proj_block, block_index_list, lens_block, moves_block = input_values
        key_value_blocks = key_value_cache[block_index_list].reshape(REQUESTS_LOCAL, LMAX, track_count)
        mixed = attend(proj_block, key_value_blocks, lens_block)
        picked = jnp.argsort(1 - moves_block, stable=True)[:MIG_DEV].astype(jnp.int32)
        entries = new_entries(proj_block[picked], lens_block[picked])
        arrived = append_cache(key_value_blocks[picked], entries, lens_block[picked], moves_block[picked] == 1)
        return (mixed, arrived)
    attended, arrived = lax.map(attend_block, (projected_rows.reshape(group_total, REQUESTS_LOCAL, FRESH_TOKENS, MERGED_COLUMNS), block_ids.reshape(group_total, REQUESTS_LOCAL, MAXB), cache_length.reshape(group_total, REQUESTS_LOCAL), moving.reshape(group_total, REQUESTS_LOCAL)))
    attended = attended.reshape(REQUEST_TOTAL, FRESH_TOKENS, QUERY_HEADS * HEAD_SIZE)
    arrived = arrived.reshape(group_total * MIG_DEV, LMAX, track_count)
    shard_cols = QUERY_HEADS * HEAD_SIZE // N_TENSOR

    def out_shard(totals, shard):
        columns = lax.dynamic_slice_in_dim(attended, shard * shard_cols, shard_cols, 2)
        weights = lax.dynamic_slice_in_dim(output_weight, shard * shard_cols, shard_cols, 0)
        partial_value = jnp.dot(columns.reshape(-1, shard_cols), weights, preferred_element_type=jnp.float32).astype(jnp.bfloat16)
        partial_value = lax.optimization_barrier(partial_value)
        return (totals + partial_value.astype(jnp.float32), None)
    totals, unused = lax.scan(out_shard, jnp.zeros((REQUEST_TOTAL * FRESH_TOKENS, EMBED_WIDTH), jnp.float32), jnp.arange(N_TENSOR, dtype=jnp.int32))
    return (totals.reshape(REQUEST_TOTAL, FRESH_TOKENS, EMBED_WIDTH).astype(jnp.bfloat16), arrived)
```

```python
import jax
import jax.numpy as jnp
from jax import lax
from jax.experimental import pallas as pl
from jax.experimental.pallas import tpu as pltpu
from jax.sharding import PartitionSpec as P

QUERY_HEADS = 32
KEY_VALUE_HEADS = 8
HEAD_SIZE = 128
MIG_DEV = 2
FRESH_PAD = 16

theta_base = 500000.0
norm_eps = 1e-05
adapter_scale = 2.0


def rotate(vectors, positions):
    half_width = vectors.shape[-1] // 2
    frequency = jnp.power(
        jnp.float32(theta_base), -jnp.arange(half_width, dtype=jnp.float32) / half_width
    )
    angles = positions.astype(jnp.float32)[..., None] * frequency
    cosine = jnp.cos(angles)
    sine = jnp.sin(angles)
    first = vectors[..., :half_width].astype(jnp.float32)
    second = vectors[..., half_width:].astype(jnp.float32)
    return jnp.concatenate(
        [first * cosine - second * sine, second * cosine + first * sine], axis=-1
    ).astype(jnp.bfloat16)


def pick_blocks(pages, cache):
    count = pages.shape[0]

    def kernel(pages_ref, cache_ref, out_ref, sem):
        def issue(i, carry):
            pltpu.make_async_copy(cache_ref.at[pages_ref[i]], out_ref.at[i], sem).start()
            return carry

        lax.fori_loop(0, count, issue, 0)
        pltpu.make_async_copy(out_ref, out_ref, sem).wait()

    return pl.pallas_call(
        kernel,
        out_shape=jax.ShapeDtypeStruct((count,) + cache.shape[1:], cache.dtype),
        in_specs=[
            pl.BlockSpec(memory_space=pltpu.SMEM),
            pl.BlockSpec(memory_space=pl.ANY),
        ],
        out_specs=pl.BlockSpec(memory_space=pl.ANY),
        scratch_shapes=[pltpu.SemaphoreType.DMA],
    )(pages, cache)


def attend(tables, lengths, moving, spots, cache, landed, queries, fresh, fresh_tokens):
    slots = lengths.shape[0]
    blocks = tables.shape[0] // slots
    block_rows, tracks = cache.shape[1:]
    span = blocks * block_rows
    sharing = QUERY_HEADS // KEY_VALUE_HEADS
    group = fresh_tokens * sharing
    query_rows = KEY_VALUE_HEADS * group
    keys = KEY_VALUE_HEADS * HEAD_SIZE
    total = span + FRESH_PAD

    def kernel(tab, lens, mov, spot, cache_ref, landed_ref, q_ref, fresh_ref, out_ref, kv, sems):
        def issue(s, carry):
            @pl.when(mov[s] == 0)
            def _():
                for b in range(blocks):
                    pltpu.make_async_copy(
                        cache_ref.at[tab[s * blocks + b]],
                        kv.at[s, pl.ds(b * block_rows, block_rows)],
                        sems.at[s],
                    ).start()

            @pl.when(mov[s] != 0)
            def _():
                pltpu.make_async_copy(
                    landed_ref.at[spot[s]], kv.at[s, pl.ds(0, span)], sems.at[s]
                ).start()

            return carry

        lax.fori_loop(0, slots, issue, 0)

        def work(s, carry):
            kv[s, pl.ds(span, FRESH_PAD), :] = fresh_ref[s]
            whole = kv.at[s, pl.ds(0, span)]
            pltpu.make_async_copy(whole, whole, sems.at[s]).wait()
            scores = []
            for h in range(KEY_VALUE_HEADS):
                q = q_ref[s, h * group : (h + 1) * group, :].astype(jnp.bfloat16)
                k = kv[s, :, h * HEAD_SIZE : (h + 1) * HEAD_SIZE]
                scores.append(
                    lax.dot_general(
                        q, k, (((1,), (1,)), ((), ())), preferred_element_type=jnp.float32
                    )
                )
            scores = jnp.concatenate(scores, axis=0) * (HEAD_SIZE ** (-0.5))
            row = lax.broadcasted_iota(jnp.int32, (query_rows, total), 0)
            col = lax.broadcasted_iota(jnp.int32, (query_rows, total), 1)
            token = lax.rem(row, group) // sharing
            valid = (col < jnp.minimum(lens[s], span)) | (
                (col >= span) & (col - span <= token)
            )
            scores = jnp.where(valid, scores, -jnp.inf)
            high = jnp.max(scores, axis=-1, keepdims=True)
            raised = jnp.exp(scores - high)
            weights = raised / jnp.sum(raised, axis=-1, keepdims=True)
            mixed = []
            for h in range(KEY_VALUE_HEADS):
                w = weights[h * group : (h + 1) * group].astype(jnp.bfloat16)
                v = kv[s, :, keys + h * HEAD_SIZE : keys + (h + 1) * HEAD_SIZE]
                mixed.append(jnp.dot(w, v, preferred_element_type=jnp.float32))
            out_ref[s] = jnp.concatenate(mixed, axis=0).astype(jnp.bfloat16)
            return carry

        lax.fori_loop(0, slots, work, 0)

    smem = pl.BlockSpec(memory_space=pltpu.SMEM)
    vmem = pl.BlockSpec(memory_space=pltpu.VMEM)
    hbm = pl.BlockSpec(memory_space=pl.ANY)
    return pl.pallas_call(
        kernel,
        out_shape=jax.ShapeDtypeStruct((slots, query_rows, HEAD_SIZE), jnp.bfloat16),
        in_specs=[smem, smem, smem, smem, hbm, hbm, vmem, vmem],
        out_specs=vmem,
        scratch_shapes=[
            pltpu.VMEM((slots, total, tracks), jnp.bfloat16),
            pltpu.SemaphoreType.DMA((slots,)),
        ],
        compiler_params=pltpu.CompilerParams(vmem_limit_bytes=40 * 1024 * 1024),
    )(tables, lengths, moving, spots, cache, landed, queries, fresh)


def per_device(
    hidden_input,
    input_norm_gain,
    merged_weight,
    output_weight,
    adapter_down,
    adapter_up,
    request_adapter,
    key_value_cache,
    block_table,
    cache_length,
    partner,
    moving,
):
    row_local, fresh_tokens, width_local = hidden_input.shape
    tensor_rank = lax.axis_index("tensor")
    replica_rank = lax.axis_index("replica")
    tensors = lax.axis_size("tensor")
    replicas = lax.axis_size("replica")
    rows = row_local * fresh_tokens
    slots = moving.shape[0]
    blocks = block_table.shape[1]
    tracks = key_value_cache.shape[2]
    span = blocks * key_value_cache.shape[1]
    column_local = merged_weight.shape[1]
    owned, rank = adapter_down.shape[:2]
    f32, bf16 = jnp.float32, jnp.bfloat16

    hidden = hidden_input.reshape(rows, width_local)
    all_rows = lax.all_gather(hidden, "replica", axis=0, tiled=True)
    gathered = lax.all_gather(hidden, "tensor", axis=1, tiled=True)

    slot_ids = jnp.arange(slots, dtype=jnp.int32)
    is_moving = moving == 1
    until = slot_ids[None, :] <= slot_ids[:, None]
    order = jnp.sum(jnp.where(until, moving[None, :], 0), axis=1) - 1
    hot = is_moving[None, :] & (order[None, :] == jnp.arange(MIG_DEV)[:, None])
    arriving = jnp.any(hot, axis=1)
    pages_out = jnp.sum(jnp.where(hot[:, :, None], block_table[None], 0), axis=1).reshape(-1)
    received = pick_blocks(pages_out, key_value_cache).reshape(MIG_DEV, span, tracks)
    flips = lax.dynamic_slice(partner, (replica_rank, tensor_rank), (1, 1))[0, 0] ^ replica_rank
    bit = 1
    while bit < replicas:
        pairs = [(i, i ^ bit) for i in range(replicas)]
        other = lax.ppermute(received, "replica", pairs)
        received = jnp.where((flips & bit) != 0, other, received)
        bit *= 2

    local_gain = lax.dynamic_slice_in_dim(
        input_norm_gain, tensor_rank * width_local, width_local, 0
    ).astype(f32)
    scaled_rows = (all_rows.astype(f32) * local_gain).astype(bf16)
    inner = jnp.einsum(
        "nd,cd->nc",
        scaled_rows,
        adapter_down.reshape(owned * rank, width_local),
        preferred_element_type=f32,
    )
    relative = jnp.repeat(request_adapter - replica_rank * owned, fresh_tokens)
    lanes = jnp.arange(owned * rank, dtype=jnp.int32)
    chosen = relative[:, None] == (lanes // rank)[None, :]
    spread = (lanes[None, :] % rank == jnp.arange(rank)[:, None]).astype(bf16)
    part = jnp.einsum(
        "rc,nc->rn", spread, jnp.where(chosen, inner, 0.0).astype(bf16), preferred_element_type=f32
    ).astype(bf16)
    parts = lax.all_gather(part, "tensor", axis=0)
    shrink_low = jnp.sum(parts.astype(f32), axis=0).astype(bf16)
    wide = jnp.einsum("rn,rc->nc", shrink_low, spread, preferred_element_type=f32)
    wide = jnp.where(chosen, wide, 0.0).astype(bf16)
    expand = jnp.dot(
        wide, adapter_up.reshape(owned * rank, column_local), preferred_element_type=f32
    ).astype(bf16)
    expand = lax.psum_scatter(expand, "replica", scatter_dimension=0, tiled=True)

    gathered_f = gathered.astype(f32)
    factor = lax.rsqrt(jnp.mean(gathered_f * gathered_f, axis=-1, keepdims=True) + norm_eps)
    scaled = (gathered_f * input_norm_gain.astype(f32)).astype(bf16)
    base = jnp.dot(scaled, merged_weight, preferred_element_type=f32)
    projected = (factor * (base + adapter_scale * expand.astype(f32))).astype(bf16)

    swapped = lax.all_to_all(
        projected.reshape(tensors, slots * fresh_tokens, column_local),
        "tensor",
        split_axis=0,
        concat_axis=0,
        tiled=True,
    )
    by_request = jnp.transpose(swapped, (1, 0, 2)).reshape(slots, fresh_tokens, -1, HEAD_SIZE)
    key_end = QUERY_HEADS + KEY_VALUE_HEADS
    positions = cache_length[:, None] + jnp.arange(fresh_tokens, dtype=jnp.int32)[None, :]
    rotated = rotate(by_request[:, :, :key_end], positions[:, :, None])
    sharing = QUERY_HEADS // KEY_VALUE_HEADS
    queries = rotated[:, :, :QUERY_HEADS].reshape(
        slots, fresh_tokens, KEY_VALUE_HEADS, sharing, HEAD_SIZE
    )
    queries = jnp.transpose(queries, (0, 2, 1, 3, 4)).reshape(slots, -1, HEAD_SIZE).astype(f32)
    entries = jnp.concatenate(
        [rotated[:, :, QUERY_HEADS:], by_request[:, :, key_end:]], axis=2
    ).reshape(slots, fresh_tokens, tracks)
    fresh = jnp.pad(entries, ((0, 0), (0, FRESH_PAD - fresh_tokens), (0, 0)))
    attended = attend(
        block_table.reshape(-1),
        cache_length,
        moving,
        jnp.clip(order, 0, MIG_DEV - 1),
        key_value_cache,
        received,
        queries,
        fresh,
        fresh_tokens,
    )
    attended = attended.reshape(slots, KEY_VALUE_HEADS, fresh_tokens, sharing * HEAD_SIZE)
    heads_local = output_weight.shape[0]
    attended = jnp.transpose(attended, (0, 2, 1, 3)).reshape(
        slots * fresh_tokens, tensors, heads_local
    )
    returned = lax.all_to_all(
        jnp.transpose(attended, (1, 0, 2)), "tensor", split_axis=0, concat_axis=0, tiled=True
    ).reshape(rows, heads_local)
    partial = jnp.dot(returned, output_weight, preferred_element_type=f32).astype(bf16)
    summed = lax.psum_scatter(partial, "tensor", scatter_dimension=1, tiled=True)

    hot_f = hot.astype(bf16)
    moved = jnp.einsum(
        "js,sc->jc", hot_f, entries.reshape(slots, -1), preferred_element_type=f32
    ).astype(bf16).reshape(MIG_DEV, fresh_tokens, tracks)
    lens = jnp.sum(jnp.where(hot, cache_length[None, :], 0), axis=1)
    places = jnp.arange(span, dtype=jnp.int32)[None, :]
    kept = jnp.where((places < lens[:, None])[:, :, None], received, jnp.zeros((), bf16))
    for offset in range(fresh_tokens):
        written = (places == lens[:, None] + offset)[:, :, None]
        kept = jnp.where(written, moved[:, offset][:, None, :], kept)
    arrived = jnp.where(arriving[:, None, None], kept, jnp.zeros((), bf16))
    return summed.reshape(row_local, fresh_tokens, -1), arrived


def solution(mesh):
    placed = (
        P("replica", None, "tensor"),
        P(),
        P(None, "tensor"),
        P("tensor", None),
        P("replica", None, "tensor"),
        P("replica", None, "tensor"),
        P(),
        P(("replica", "tensor"), None, None),
        P(("replica", "tensor"), None),
        P(("replica", "tensor")),
        P(),
        P(("replica", "tensor")),
    )
    return jax.shard_map(
        per_device,
        mesh=mesh,
        in_specs=placed,
        out_specs=(P("replica", None, "tensor"), P(("replica", "tensor"), None, None)),
        check_vma=False,
    )
```

```python
import jax
import jax.numpy as jnp
from jax import lax
from jax.experimental import pallas as pl
from jax.experimental.pallas import tpu as pltpu
from jax.sharding import PartitionSpec as P

QUERY_HEADS = 32
KEY_VALUE_HEADS = 8
HEAD_SIZE = 128
MIG_DEV = 2
FRESH_PAD = 16

theta_base = 500000.0
norm_eps = 1e-05
adapter_scale = 2.0


def rotate(vectors, positions):
    half_width = vectors.shape[-1] // 2
    frequency = jnp.power(
        jnp.float32(theta_base), -jnp.arange(half_width, dtype=jnp.float32) / half_width
    )
    angles = positions.astype(jnp.float32)[..., None] * frequency
    cosine = jnp.cos(angles)
    sine = jnp.sin(angles)
    first = vectors[..., :half_width].astype(jnp.float32)
    second = vectors[..., half_width:].astype(jnp.float32)
    return jnp.concatenate(
        [first * cosine - second * sine, second * cosine + first * sine], axis=-1
    ).astype(jnp.bfloat16)


def pick_blocks(pages, cache):
    count = pages.shape[0]

    def kernel(pages_ref, cache_ref, out_ref, sem):
        def issue(i, carry):
            pltpu.make_async_copy(cache_ref.at[pages_ref[i]], out_ref.at[i], sem).start()
            return carry

        lax.fori_loop(0, count, issue, 0)
        pltpu.make_async_copy(out_ref, out_ref, sem).wait()

    return pl.pallas_call(
        kernel,
        out_shape=jax.ShapeDtypeStruct((count,) + cache.shape[1:], cache.dtype),
        in_specs=[
            pl.BlockSpec(memory_space=pltpu.SMEM),
            pl.BlockSpec(memory_space=pl.ANY),
        ],
        out_specs=pl.BlockSpec(memory_space=pltpu.VMEM),
        scratch_shapes=[pltpu.SemaphoreType.DMA],
        compiler_params=pltpu.CompilerParams(vmem_limit_bytes=16 * 1024 * 1024),
    )(pages, cache)


def project_out(values, weight, tensors):
    rows, depth = values.shape
    width = weight.shape[1] // tensors
    chips = tensors // 2
    tile = 256
    turns = list(range(1, chips)) + [0]
    bf16, f32 = jnp.bfloat16, jnp.float32

    def kernel(a_ref, w_ref, out_ref, theirs, got, merged, landed, acc, ps, pr, cs, cr):
        me = lax.axis_index("tensor")
        core = lax.rem(me, 2)
        chip = me // 2
        sibling = me + 1 - 2 * core
        others = [lax.rem(chip + d, chips) * 2 + core for d in range(1, chips)]
        barrier = pltpu.get_barrier_semaphore()
        for peer in [sibling] + others:
            pl.semaphore_signal(
                barrier,
                inc=1,
                device_id={"tensor": peer},
                device_id_type=pl.DeviceIdType.MESH,
            )
        pl.semaphore_wait(barrier, chips)

        def columns(owner, j):
            return pl.ds(pl.multiple_of(owner * width + j * tile, tile), tile)

        def here(j):
            return pl.ds(pl.multiple_of(j * tile, tile), tile)

        first, second = [], []
        for i, d in enumerate(turns):
            owner = lax.rem(chip + d, chips) * 2 + 1 - core

            @pl.loop(0, width // tile)
            def _(j, i=i, owner=owner):
                theirs[i, :, here(j)] = jnp.dot(
                    a_ref[...], w_ref[:, columns(owner, j)], preferred_element_type=f32
                ).astype(bf16)

            copy = pltpu.make_async_remote_copy(
                src_ref=theirs.at[i],
                dst_ref=got.at[i],
                send_sem=ps.at[i],
                recv_sem=pr.at[i],
                device_id={"tensor": sibling},
                device_id_type=pl.DeviceIdType.MESH,
            )
            copy.start()
            first.append(copy)
        for i, d in enumerate(turns):
            owner = lax.rem(chip + d, chips) * 2 + core
            first[i].wait_recv()

            @pl.loop(0, width // tile)
            def _(j, i=i, d=d, owner=owner):
                own = jnp.dot(
                    a_ref[...], w_ref[:, columns(owner, j)], preferred_element_type=f32
                )
                pair = own + got[i, :, here(j)].astype(f32)
                if d == 0:
                    acc[:, here(j)] = pair
                else:
                    merged[i, :, here(j)] = pair.astype(bf16)

            if d != 0:
                copy = pltpu.make_async_remote_copy(
                    src_ref=merged.at[i],
                    dst_ref=landed.at[i],
                    send_sem=cs.at[i],
                    recv_sem=cr.at[i],
                    device_id={"tensor": owner},
                    device_id_type=pl.DeviceIdType.MESH,
                )
                copy.start()
                second.append(copy)
        for copy in second:
            copy.wait_recv()

        @pl.loop(0, width // tile)
        def _(j):
            total = acc[:, here(j)]
            for i in range(chips - 1):
                total = total + landed[i, :, here(j)].astype(f32)
            out_ref[:, here(j)] = total.astype(bf16)

        for copy in first + second:
            copy.wait_send()

    vmem = pl.BlockSpec(memory_space=pltpu.VMEM)
    return pl.pallas_call(
        kernel,
        out_shape=jax.ShapeDtypeStruct((rows, width), bf16),
        in_specs=[vmem, vmem],
        out_specs=vmem,
        scratch_shapes=[
            pltpu.VMEM((chips, rows, width), bf16),
            pltpu.VMEM((chips, rows, width), bf16),
            pltpu.VMEM((chips - 1, rows, width), bf16),
            pltpu.VMEM((chips - 1, rows, width), bf16),
            pltpu.VMEM((rows, width), f32),
            pltpu.SemaphoreType.DMA((chips,)),
            pltpu.SemaphoreType.DMA((chips,)),
            pltpu.SemaphoreType.DMA((chips - 1,)),
            pltpu.SemaphoreType.DMA((chips - 1,)),
        ],
        compiler_params=pltpu.CompilerParams(
            collective_id=0, has_side_effects=True, vmem_limit_bytes=36 * 1024 * 1024
        ),
    )(values, weight)


def attend(tables, lengths, moving, spots, cache, landed, queries, fresh, fresh_tokens):
    slots = lengths.shape[0]
    blocks = tables.shape[0] // slots
    block_rows, tracks = cache.shape[1:]
    span = blocks * block_rows
    sharing = QUERY_HEADS // KEY_VALUE_HEADS
    group = fresh_tokens * sharing
    query_rows = KEY_VALUE_HEADS * group
    keys = KEY_VALUE_HEADS * HEAD_SIZE
    total = span + FRESH_PAD

    def kernel(tab, lens, mov, spot, cache_ref, landed_ref, q_ref, fresh_ref, out_ref, kv, sems):
        def issue(s, carry):
            @pl.when(mov[s] == 0)
            def _():
                for b in range(blocks):
                    pltpu.make_async_copy(
                        cache_ref.at[tab[s * blocks + b]],
                        kv.at[s, pl.ds(b * block_rows, block_rows)],
                        sems.at[s],
                    ).start()

            @pl.when(mov[s] != 0)
            def _():
                pltpu.make_async_copy(
                    landed_ref.at[spot[s]], kv.at[s, pl.ds(0, span)], sems.at[s]
                ).start()

            return carry

        lax.fori_loop(0, slots, issue, 0)

        def work(s, carry):
            kv[s, pl.ds(span, FRESH_PAD), :] = fresh_ref[s]
            whole = kv.at[s, pl.ds(0, span)]
            pltpu.make_async_copy(whole, whole, sems.at[s]).wait()
            scores = []
            for h in range(KEY_VALUE_HEADS):
                q = q_ref[s, h * group : (h + 1) * group, :].astype(jnp.bfloat16)
                k = kv[s, :, h * HEAD_SIZE : (h + 1) * HEAD_SIZE]
                scores.append(
                    lax.dot_general(
                        q, k, (((1,), (1,)), ((), ())), preferred_element_type=jnp.float32
                    )
                )
            scores = jnp.concatenate(scores, axis=0) * (HEAD_SIZE ** (-0.5))
            row = lax.broadcasted_iota(jnp.int32, (query_rows, total), 0)
            col = lax.broadcasted_iota(jnp.int32, (query_rows, total), 1)
            token = lax.rem(row, group) // sharing
            valid = (col < jnp.minimum(lens[s], span)) | (
                (col >= span) & (col - span <= token)
            )
            scores = jnp.where(valid, scores, -jnp.inf)
            high = jnp.max(scores, axis=-1, keepdims=True)
            raised = jnp.exp(scores - high)
            weights = raised / jnp.sum(raised, axis=-1, keepdims=True)
            mixed = []
            for h in range(KEY_VALUE_HEADS):
                w = weights[h * group : (h + 1) * group].astype(jnp.bfloat16)
                v = kv[s, :, keys + h * HEAD_SIZE : keys + (h + 1) * HEAD_SIZE]
                mixed.append(jnp.dot(w, v, preferred_element_type=jnp.float32))
            out_ref[s] = jnp.concatenate(mixed, axis=0).astype(jnp.bfloat16)
            return carry

        lax.fori_loop(0, slots, work, 0)

    smem = pl.BlockSpec(memory_space=pltpu.SMEM)
    vmem = pl.BlockSpec(memory_space=pltpu.VMEM)
    hbm = pl.BlockSpec(memory_space=pl.ANY)
    return pl.pallas_call(
        kernel,
        out_shape=jax.ShapeDtypeStruct((slots, query_rows, HEAD_SIZE), jnp.bfloat16),
        in_specs=[smem, smem, smem, smem, hbm, hbm, vmem, vmem],
        out_specs=vmem,
        scratch_shapes=[
            pltpu.VMEM((slots, total, tracks), jnp.bfloat16),
            pltpu.SemaphoreType.DMA((slots,)),
        ],
        compiler_params=pltpu.CompilerParams(vmem_limit_bytes=40 * 1024 * 1024),
    )(tables, lengths, moving, spots, cache, landed, queries, fresh)


def per_device(
    hidden_input,
    input_norm_gain,
    merged_weight,
    output_weight,
    adapter_down,
    adapter_up,
    request_adapter,
    key_value_cache,
    block_table,
    cache_length,
    partner,
    moving,
):
    row_local, fresh_tokens, width_local = hidden_input.shape
    tensor_rank = lax.axis_index("tensor")
    replica_rank = lax.axis_index("replica")
    tensors = lax.axis_size("tensor")
    replicas = lax.axis_size("replica")
    rows = row_local * fresh_tokens
    slots = moving.shape[0]
    blocks = block_table.shape[1]
    tracks = key_value_cache.shape[2]
    span = blocks * key_value_cache.shape[1]
    column_local = merged_weight.shape[1]
    owned, rank = adapter_down.shape[:2]
    f32, bf16 = jnp.float32, jnp.bfloat16

    hidden = hidden_input.reshape(rows, width_local)
    all_rows = lax.all_gather(hidden, "replica", axis=0, tiled=True)
    gathered = lax.all_gather(hidden, "tensor", axis=1, tiled=True)

    slot_ids = jnp.arange(slots, dtype=jnp.int32)
    is_moving = moving == 1
    until = slot_ids[None, :] <= slot_ids[:, None]
    order = jnp.sum(jnp.where(until, moving[None, :], 0), axis=1) - 1
    hot = is_moving[None, :] & (order[None, :] == jnp.arange(MIG_DEV)[:, None])
    arriving = jnp.any(hot, axis=1)
    pages_out = jnp.sum(jnp.where(hot[:, :, None], block_table[None], 0), axis=1).reshape(-1)
    received = pick_blocks(pages_out, key_value_cache).reshape(MIG_DEV, span, tracks)
    flips = lax.dynamic_slice(partner, (replica_rank, tensor_rank), (1, 1))[0, 0] ^ replica_rank
    hops = [1 << i for i in range((replicas - 1).bit_length())]

    def hop(held, bit):
        pairs = [(i, i ^ bit) for i in range(replicas)]
        other = lax.ppermute(held, "replica", pairs)
        return jnp.where((flips & bit) != 0, other, held)

    local_gain = lax.dynamic_slice_in_dim(
        input_norm_gain, tensor_rank * width_local, width_local, 0
    ).astype(f32)
    local_gain, received = lax.optimization_barrier((local_gain, received))
    scaled_rows = (all_rows.astype(f32) * local_gain).astype(bf16)
    inner = jnp.einsum(
        "nd,cd->nc",
        scaled_rows,
        adapter_down.reshape(owned * rank, width_local),
        preferred_element_type=f32,
    )
    relative = jnp.repeat(request_adapter - replica_rank * owned, fresh_tokens)
    lanes = jnp.arange(owned * rank, dtype=jnp.int32)
    chosen = relative[:, None] == (lanes // rank)[None, :]
    spread = (lanes[None, :] % rank == jnp.arange(rank)[:, None]).astype(bf16)
    part = jnp.einsum(
        "rc,nc->rn", spread, jnp.where(chosen, inner, 0.0).astype(bf16), preferred_element_type=f32
    ).astype(bf16)
    parts = lax.all_gather(part, "tensor", axis=0)
    received = hop(received, hops[0])
    parts, received, gathered = lax.optimization_barrier((parts, received, gathered))
    shrink_low = jnp.sum(parts.astype(f32), axis=0).astype(bf16)
    wide = jnp.einsum("rn,rc->nc", shrink_low, spread, preferred_element_type=f32)
    wide = jnp.where(chosen, wide, 0.0).astype(bf16)
    expand = jnp.dot(
        wide, adapter_up.reshape(owned * rank, column_local), preferred_element_type=f32
    ).astype(bf16)
    expand = lax.psum_scatter(expand, "replica", scatter_dimension=0, tiled=True)
    for bit in hops[1:]:
        received = hop(received, bit)
    expand, received = lax.optimization_barrier((expand, received))

    gathered_f = gathered.astype(f32)
    factor = lax.rsqrt(jnp.mean(gathered_f * gathered_f, axis=-1, keepdims=True) + norm_eps)
    scaled = (gathered_f * input_norm_gain.astype(f32)).astype(bf16)
    base = jnp.dot(scaled, merged_weight, preferred_element_type=f32)
    projected = (factor * (base + adapter_scale * expand.astype(f32))).astype(bf16)

    swapped = lax.all_to_all(
        projected.reshape(tensors, slots * fresh_tokens, column_local),
        "tensor",
        split_axis=0,
        concat_axis=0,
        tiled=True,
    )
    by_request = jnp.transpose(swapped, (1, 0, 2)).reshape(slots, fresh_tokens, -1, HEAD_SIZE)
    key_end = QUERY_HEADS + KEY_VALUE_HEADS
    positions = cache_length[:, None] + jnp.arange(fresh_tokens, dtype=jnp.int32)[None, :]
    rotated = rotate(by_request[:, :, :key_end], positions[:, :, None])
    sharing = QUERY_HEADS // KEY_VALUE_HEADS
    queries = rotated[:, :, :QUERY_HEADS].reshape(
        slots, fresh_tokens, KEY_VALUE_HEADS, sharing, HEAD_SIZE
    )
    queries = jnp.transpose(queries, (0, 2, 1, 3, 4)).reshape(slots, -1, HEAD_SIZE).astype(f32)
    entries = jnp.concatenate(
        [rotated[:, :, QUERY_HEADS:], by_request[:, :, key_end:]], axis=2
    ).reshape(slots, fresh_tokens, tracks)
    fresh = jnp.pad(entries, ((0, 0), (0, FRESH_PAD - fresh_tokens), (0, 0)))
    attended = attend(
        block_table.reshape(-1),
        cache_length,
        moving,
        jnp.clip(order, 0, MIG_DEV - 1),
        key_value_cache,
        received,
        queries,
        fresh,
        fresh_tokens,
    )
    attended = attended.reshape(slots, KEY_VALUE_HEADS, fresh_tokens, sharing * HEAD_SIZE)
    heads_local = output_weight.shape[0]
    attended = jnp.transpose(attended, (0, 2, 1, 3)).reshape(
        slots * fresh_tokens, tensors, heads_local
    )
    returned = lax.all_to_all(
        jnp.transpose(attended, (1, 0, 2)), "tensor", split_axis=0, concat_axis=0, tiled=True
    ).reshape(rows, heads_local)
    summed = project_out(returned, output_weight, tensors)

    hot_f = hot.astype(bf16)
    moved = jnp.einsum(
        "js,sc->jc", hot_f, entries.reshape(slots, -1), preferred_element_type=f32
    ).astype(bf16).reshape(MIG_DEV, fresh_tokens, tracks)
    lens = jnp.sum(jnp.where(hot, cache_length[None, :], 0), axis=1)
    places = jnp.arange(span, dtype=jnp.int32)[None, :]
    kept = jnp.where((places < lens[:, None])[:, :, None], received, jnp.zeros((), bf16))
    for offset in range(fresh_tokens):
        written = (places == lens[:, None] + offset)[:, :, None]
        kept = jnp.where(written, moved[:, offset][:, None, :], kept)
    arrived = jnp.where(arriving[:, None, None], kept, jnp.zeros((), bf16))
    return summed.reshape(row_local, fresh_tokens, -1), arrived


def solution(mesh):
    placed = (
        P("replica", None, "tensor"),
        P(),
        P(None, "tensor"),
        P("tensor", None),
        P("replica", None, "tensor"),
        P("replica", None, "tensor"),
        P(),
        P(("replica", "tensor"), None, None),
        P(("replica", "tensor"), None),
        P(("replica", "tensor")),
        P(),
        P(("replica", "tensor")),
    )
    return jax.shard_map(
        per_device,
        mesh=mesh,
        in_specs=placed,
        out_specs=(P("replica", None, "tensor"), P(("replica", "tensor"), None, None)),
        check_vma=False,
    )
```

```python
import jax
import jax.numpy as jnp
from jax import lax
from jax.experimental import pallas as pl
from jax.experimental.pallas import tpu as pltpu
from jax.sharding import PartitionSpec as P

QUERY_HEADS = 32
KEY_VALUE_HEADS = 8
HEAD_SIZE = 128
MIG_DEV = 2
FRESH_PAD = 16

theta_base = 500000.0
norm_eps = 1e-05
adapter_scale = 2.0


def rotate(vectors, positions):
    half_width = vectors.shape[-1] // 2
    frequency = jnp.power(
        jnp.float32(theta_base), -jnp.arange(half_width, dtype=jnp.float32) / half_width
    )
    angles = positions.astype(jnp.float32)[..., None] * frequency
    cosine = jnp.cos(angles)
    sine = jnp.sin(angles)
    first = vectors[..., :half_width].astype(jnp.float32)
    second = vectors[..., half_width:].astype(jnp.float32)
    return jnp.concatenate(
        [first * cosine - second * sine, second * cosine + first * sine], axis=-1
    ).astype(jnp.bfloat16)


def pick_blocks(pages, cache):
    count = pages.shape[0]

    def kernel(pages_ref, cache_ref, out_ref, sem):
        def issue(i, carry):
            pltpu.make_async_copy(cache_ref.at[pages_ref[i]], out_ref.at[i], sem).start()
            return carry

        lax.fori_loop(0, count, issue, 0)
        pltpu.make_async_copy(out_ref, out_ref, sem).wait()

    return pl.pallas_call(
        kernel,
        out_shape=jax.ShapeDtypeStruct((count,) + cache.shape[1:], cache.dtype),
        in_specs=[
            pl.BlockSpec(memory_space=pltpu.SMEM),
            pl.BlockSpec(memory_space=pl.ANY),
        ],
        out_specs=pl.BlockSpec(memory_space=pltpu.VMEM),
        scratch_shapes=[pltpu.SemaphoreType.DMA],
        compiler_params=pltpu.CompilerParams(vmem_limit_bytes=16 * 1024 * 1024),
    )(pages, cache)


def project_out(values, weight, tensors):
    rows, depth = values.shape
    width = weight.shape[1] // tensors
    chips = tensors // 2
    tile = 256
    turns = list(range(1, chips)) + [0]
    bf16, f32 = jnp.bfloat16, jnp.float32

    def kernel(a_ref, w_ref, out_ref, theirs, got, merged, landed, acc, ps, pr, cs, cr):
        me = lax.axis_index("tensor")
        core = lax.rem(me, 2)
        chip = me // 2
        sibling = me + 1 - 2 * core
        others = [lax.rem(chip + d, chips) * 2 + core for d in range(1, chips)]
        barrier = pltpu.get_barrier_semaphore()
        for peer in [sibling] + others:
            pl.semaphore_signal(
                barrier,
                inc=1,
                device_id={"tensor": peer},
                device_id_type=pl.DeviceIdType.MESH,
            )
        pl.semaphore_wait(barrier, chips)

        def columns(owner, j):
            return pl.ds(pl.multiple_of(owner * width + j * tile, tile), tile)

        def here(j):
            return pl.ds(pl.multiple_of(j * tile, tile), tile)

        first, second = [], []
        for i, d in enumerate(turns):
            owner = lax.rem(chip + d, chips) * 2 + 1 - core

            @pl.loop(0, width // tile)
            def _(j, i=i, owner=owner):
                theirs[i, :, here(j)] = jnp.dot(
                    a_ref[...], w_ref[:, columns(owner, j)], preferred_element_type=f32
                ).astype(bf16)

            copy = pltpu.make_async_remote_copy(
                src_ref=theirs.at[i],
                dst_ref=got.at[i],
                send_sem=ps.at[i],
                recv_sem=pr.at[i],
                device_id={"tensor": sibling},
                device_id_type=pl.DeviceIdType.MESH,
            )
            copy.start()
            first.append(copy)
        for i, d in enumerate(turns):
            owner = lax.rem(chip + d, chips) * 2 + core
            first[i].wait_recv()

            @pl.loop(0, width // tile)
            def _(j, i=i, d=d, owner=owner):
                own = jnp.dot(
                    a_ref[...], w_ref[:, columns(owner, j)], preferred_element_type=f32
                )
                pair = own + got[i, :, here(j)].astype(f32)
                if d == 0:
                    acc[:, here(j)] = pair
                else:
                    merged[i, :, here(j)] = pair.astype(bf16)

            if d != 0:
                copy = pltpu.make_async_remote_copy(
                    src_ref=merged.at[i],
                    dst_ref=landed.at[i],
                    send_sem=cs.at[i],
                    recv_sem=cr.at[i],
                    device_id={"tensor": owner},
                    device_id_type=pl.DeviceIdType.MESH,
                )
                copy.start()
                second.append(copy)
        for copy in second:
            copy.wait_recv()

        @pl.loop(0, width // tile)
        def _(j):
            total = acc[:, here(j)]
            for i in range(chips - 1):
                total = total + landed[i, :, here(j)].astype(f32)
            out_ref[:, here(j)] = total.astype(bf16)

        for copy in first + second:
            copy.wait_send()

    vmem = pl.BlockSpec(memory_space=pltpu.VMEM)
    return pl.pallas_call(
        kernel,
        out_shape=jax.ShapeDtypeStruct((rows, width), bf16),
        in_specs=[vmem, vmem],
        out_specs=vmem,
        scratch_shapes=[
            pltpu.VMEM((chips, rows, width), bf16),
            pltpu.VMEM((chips, rows, width), bf16),
            pltpu.VMEM((chips - 1, rows, width), bf16),
            pltpu.VMEM((chips - 1, rows, width), bf16),
            pltpu.VMEM((rows, width), f32),
            pltpu.SemaphoreType.DMA((chips,)),
            pltpu.SemaphoreType.DMA((chips,)),
            pltpu.SemaphoreType.DMA((chips - 1,)),
            pltpu.SemaphoreType.DMA((chips - 1,)),
        ],
        compiler_params=pltpu.CompilerParams(
            collective_id=0, has_side_effects=True, vmem_limit_bytes=30 * 1024 * 1024
        ),
    )(values, weight)


def attend(tables, lengths, moving, spots, cache, landed, queries, fresh, fresh_tokens):
    slots = lengths.shape[0]
    blocks = tables.shape[0] // slots
    block_rows, tracks = cache.shape[1:]
    span = blocks * block_rows
    sharing = QUERY_HEADS // KEY_VALUE_HEADS
    group = fresh_tokens * sharing
    query_rows = KEY_VALUE_HEADS * group
    keys = KEY_VALUE_HEADS * HEAD_SIZE
    total = span + FRESH_PAD

    def kernel(tab, lens, mov, spot, cache_ref, landed_ref, q_ref, fresh_ref, out_ref, kv, sems):
        def issue(s, carry):
            @pl.when(mov[s] == 0)
            def _():
                for b in range(blocks):
                    pltpu.make_async_copy(
                        cache_ref.at[tab[s * blocks + b]],
                        kv.at[s, pl.ds(b * block_rows, block_rows)],
                        sems.at[s],
                    ).start()

            @pl.when(mov[s] != 0)
            def _():
                pltpu.make_async_copy(
                    landed_ref.at[spot[s]], kv.at[s, pl.ds(0, span)], sems.at[s]
                ).start()

            return carry

        lax.fori_loop(0, slots, issue, 0)

        def work(s, carry):
            kv[s, pl.ds(span, FRESH_PAD), :] = fresh_ref[s]
            whole = kv.at[s, pl.ds(0, span)]
            pltpu.make_async_copy(whole, whole, sems.at[s]).wait()
            scores = []
            for h in range(KEY_VALUE_HEADS):
                q = q_ref[s, h * group : (h + 1) * group, :].astype(jnp.bfloat16)
                k = kv[s, :, h * HEAD_SIZE : (h + 1) * HEAD_SIZE]
                scores.append(
                    lax.dot_general(
                        q, k, (((1,), (1,)), ((), ())), preferred_element_type=jnp.float32
                    )
                )
            scores = jnp.concatenate(scores, axis=0) * (HEAD_SIZE ** (-0.5))
            row = lax.broadcasted_iota(jnp.int32, (query_rows, total), 0)
            col = lax.broadcasted_iota(jnp.int32, (query_rows, total), 1)
            token = lax.rem(row, group) // sharing
            valid = (col < jnp.minimum(lens[s], span)) | (
                (col >= span) & (col - span <= token)
            )
            scores = jnp.where(valid, scores, -jnp.inf)
            high = jnp.max(scores, axis=-1, keepdims=True)
            raised = jnp.exp(scores - high)
            weights = raised / jnp.sum(raised, axis=-1, keepdims=True)
            mixed = []
            for h in range(KEY_VALUE_HEADS):
                w = weights[h * group : (h + 1) * group].astype(jnp.bfloat16)
                v = kv[s, :, keys + h * HEAD_SIZE : keys + (h + 1) * HEAD_SIZE]
                mixed.append(jnp.dot(w, v, preferred_element_type=jnp.float32))
            out_ref[s] = jnp.concatenate(mixed, axis=0).astype(jnp.bfloat16)
            return carry

        lax.fori_loop(0, slots, work, 0)

    smem = pl.BlockSpec(memory_space=pltpu.SMEM)
    vmem = pl.BlockSpec(memory_space=pltpu.VMEM)
    hbm = pl.BlockSpec(memory_space=pl.ANY)
    return pl.pallas_call(
        kernel,
        out_shape=jax.ShapeDtypeStruct((slots, query_rows, HEAD_SIZE), jnp.bfloat16),
        in_specs=[smem, smem, smem, smem, hbm, hbm, vmem, vmem],
        out_specs=vmem,
        scratch_shapes=[
            pltpu.VMEM((slots, total, tracks), jnp.bfloat16),
            pltpu.SemaphoreType.DMA((slots,)),
        ],
        compiler_params=pltpu.CompilerParams(vmem_limit_bytes=22 * 1024 * 1024),
    )(tables, lengths, moving, spots, cache, landed, queries, fresh)


def per_device(
    hidden_input,
    input_norm_gain,
    merged_weight,
    output_weight,
    adapter_down,
    adapter_up,
    request_adapter,
    key_value_cache,
    block_table,
    cache_length,
    partner,
    moving,
):
    row_local, fresh_tokens, width_local = hidden_input.shape
    tensor_rank = lax.axis_index("tensor")
    replica_rank = lax.axis_index("replica")
    tensors = lax.axis_size("tensor")
    replicas = lax.axis_size("replica")
    rows = row_local * fresh_tokens
    slots = moving.shape[0]
    blocks = block_table.shape[1]
    tracks = key_value_cache.shape[2]
    span = blocks * key_value_cache.shape[1]
    column_local = merged_weight.shape[1]
    owned, rank = adapter_down.shape[:2]
    f32, bf16 = jnp.float32, jnp.bfloat16

    hidden = hidden_input.reshape(rows, width_local)
    all_rows = lax.all_gather(hidden, "replica", axis=0, tiled=True)
    gathered = lax.all_gather(hidden, "tensor", axis=1, tiled=True)

    slot_ids = jnp.arange(slots, dtype=jnp.int32)
    is_moving = moving == 1
    until = slot_ids[None, :] <= slot_ids[:, None]
    order = jnp.sum(jnp.where(until, moving[None, :], 0), axis=1) - 1
    hot = is_moving[None, :] & (order[None, :] == jnp.arange(MIG_DEV)[:, None])
    arriving = jnp.any(hot, axis=1)
    pages_out = jnp.sum(jnp.where(hot[:, :, None], block_table[None], 0), axis=1).reshape(-1)
    received = pick_blocks(pages_out, key_value_cache).reshape(MIG_DEV, span, tracks)
    flips = lax.dynamic_slice(partner, (replica_rank, tensor_rank), (1, 1))[0, 0] ^ replica_rank
    hops = [1 << i for i in range((replicas - 1).bit_length())]

    def hop(held, bit):
        pairs = [(i, i ^ bit) for i in range(replicas)]
        other = lax.ppermute(held, "replica", pairs)
        return jnp.where((flips & bit) != 0, other, held)

    local_gain = lax.dynamic_slice_in_dim(
        input_norm_gain, tensor_rank * width_local, width_local, 0
    ).astype(f32)
    all_rows, received = lax.optimization_barrier((all_rows, received))
    scaled_rows = (all_rows.astype(f32) * local_gain).astype(bf16)
    inner = jnp.einsum(
        "nd,cd->nc",
        scaled_rows,
        adapter_down.reshape(owned * rank, width_local),
        preferred_element_type=f32,
    )
    relative = jnp.repeat(request_adapter - replica_rank * owned, fresh_tokens)
    lanes = jnp.arange(owned * rank, dtype=jnp.int32)
    chosen = relative[:, None] == (lanes // rank)[None, :]
    spread = (lanes[None, :] % rank == jnp.arange(rank)[:, None]).astype(bf16)
    part = jnp.einsum(
        "rc,nc->rn", spread, jnp.where(chosen, inner, 0.0).astype(bf16), preferred_element_type=f32
    ).astype(bf16)
    parts = lax.all_gather(part, "tensor", axis=0)
    for bit in hops:
        received = hop(received, bit)
    parts, received, gathered = lax.optimization_barrier((parts, received, gathered))
    shrink_low = jnp.sum(parts.astype(f32), axis=0).astype(bf16)
    wide = jnp.einsum("rn,rc->nc", shrink_low, spread, preferred_element_type=f32)
    wide = jnp.where(chosen, wide, 0.0).astype(bf16)
    expand = jnp.dot(
        wide, adapter_up.reshape(owned * rank, column_local), preferred_element_type=f32
    ).astype(bf16)
    expand = lax.psum_scatter(expand, "replica", scatter_dimension=0, tiled=True)

    gathered_f = gathered.astype(f32)
    factor = lax.rsqrt(jnp.mean(gathered_f * gathered_f, axis=-1, keepdims=True) + norm_eps)
    scaled = (gathered_f * input_norm_gain.astype(f32)).astype(bf16)
    base = jnp.dot(scaled, merged_weight, preferred_element_type=f32)
    projected = (factor * (base + adapter_scale * expand.astype(f32))).astype(bf16)

    swapped = lax.all_to_all(
        projected.reshape(tensors, slots * fresh_tokens, column_local),
        "tensor",
        split_axis=0,
        concat_axis=0,
        tiled=True,
    )
    by_request = jnp.transpose(swapped, (1, 0, 2)).reshape(slots, fresh_tokens, -1, HEAD_SIZE)
    key_end = QUERY_HEADS + KEY_VALUE_HEADS
    positions = cache_length[:, None] + jnp.arange(fresh_tokens, dtype=jnp.int32)[None, :]
    rotated = rotate(by_request[:, :, :key_end], positions[:, :, None])
    sharing = QUERY_HEADS // KEY_VALUE_HEADS
    queries = rotated[:, :, :QUERY_HEADS].reshape(
        slots, fresh_tokens, KEY_VALUE_HEADS, sharing, HEAD_SIZE
    )
    queries = jnp.transpose(queries, (0, 2, 1, 3, 4)).reshape(slots, -1, HEAD_SIZE).astype(f32)
    entries = jnp.concatenate(
        [rotated[:, :, QUERY_HEADS:], by_request[:, :, key_end:]], axis=2
    ).reshape(slots, fresh_tokens, tracks)
    fresh = jnp.pad(entries, ((0, 0), (0, FRESH_PAD - fresh_tokens), (0, 0)))
    attended = attend(
        block_table.reshape(-1),
        cache_length,
        moving,
        jnp.clip(order, 0, MIG_DEV - 1),
        key_value_cache,
        received,
        queries,
        fresh,
        fresh_tokens,
    )
    attended = attended.reshape(slots, KEY_VALUE_HEADS, fresh_tokens, sharing * HEAD_SIZE)
    heads_local = output_weight.shape[0]
    attended = jnp.transpose(attended, (0, 2, 1, 3)).reshape(
        slots * fresh_tokens, tensors, heads_local
    )
    returned = lax.all_to_all(
        jnp.transpose(attended, (1, 0, 2)), "tensor", split_axis=0, concat_axis=0, tiled=True
    ).reshape(rows, heads_local)
    summed = project_out(returned, output_weight, tensors)

    hot_f = hot.astype(bf16)
    moved = jnp.einsum(
        "js,sc->jc", hot_f, entries.reshape(slots, -1), preferred_element_type=f32
    ).astype(bf16).reshape(MIG_DEV, fresh_tokens, tracks)
    lens = jnp.sum(jnp.where(hot, cache_length[None, :], 0), axis=1)
    places = jnp.arange(span, dtype=jnp.int32)[None, :]
    kept = jnp.where((places < lens[:, None])[:, :, None], received, jnp.zeros((), bf16))
    for offset in range(fresh_tokens):
        written = (places == lens[:, None] + offset)[:, :, None]
        kept = jnp.where(written, moved[:, offset][:, None, :], kept)
    arrived = jnp.where(arriving[:, None, None], kept, jnp.zeros((), bf16))
    return summed.reshape(row_local, fresh_tokens, -1), arrived


def solution(mesh):
    placed = (
        P("replica", None, "tensor"),
        P(),
        P(None, "tensor"),
        P("tensor", None),
        P("replica", None, "tensor"),
        P("replica", None, "tensor"),
        P(),
        P(("replica", "tensor"), None, None),
        P(("replica", "tensor"), None),
        P(("replica", "tensor")),
        P(),
        P(("replica", "tensor")),
    )
    return jax.shard_map(
        per_device,
        mesh=mesh,
        in_specs=placed,
        out_specs=(P("replica", None, "tensor"), P(("replica", "tensor"), None, None)),
        check_vma=False,
    )
```
